512 devices in a mesh: feat: 16 (over x_hi, y), ex: 32 (over z, x_lo, core).
Axes of the slice: x: 4 (x_hi: 2, x_lo: 2; x = x_hi * 2 + x_lo), y: 8, z: 8, core: 2. Of those that a mesh axis runs over, the one named last changes fastest.
Arguments:
- train_grads: bfloat16 [4096, 262144], P('ex', 'feat')
- target_grads: bfloat16 [1024, 262144], P('ex', 'feat')
- signs: int32 [32, 8192], replicated, may hold values from -1 to 1, as said below
- block_order: int32 [32], replicated, may hold values from 0 to 31, each once
Outputs:
- train_features: bfloat16 [4096, 8192], P('ex', 'feat')
- cosines: float32 [4096, 32, 32], P('ex', None, 'feat')
The draws below stay inside these ranges and needn't reach their ends.
Inputs may be any that keep to these rules, and one draw needn't show every extreme that they name: `signs`: every entry is +1 or -1.
All inputs are finite; a program needn't handle non-finite values.
Results may differ from the reference program's by a relative error of at most 0.013.
Values may be sent and summed in bfloat16 or wider, within the bound.
A program may use at most 64 MiB of HBM per device.

```python
import math
import jax
import jax.numpy as jnp
from jax import lax

P_SIZE = 8192
TGT_DEV = 32
F = 262144
NBLK = 32
EXAMPLES = 4096
TARGETS = 1024
N_EX = 32


def shared_directions(key):
    return jax.random.normal(jax.random.fold_in(key, 11), (4, F), jnp.float32)


def draw_train_grads(key, part):
    directions = shared_directions(key)
    key = jax.random.fold_in(key, 1)
    pick_key, noise_key = jax.random.split(key, 2)
    picks = jax.random.randint(pick_key, (EXAMPLES,), 0, 4)
    noise = jax.random.normal(noise_key, (EXAMPLES, F), jnp.float32)
    return (noise + 0.8 * directions[picks]).astype(jnp.bfloat16)


def draw_target_grads(key, part):
    directions = shared_directions(key)
    key = jax.random.fold_in(key, 2)
    pick_key, noise_key = jax.random.split(key, 2)
    picks = jax.random.randint(pick_key, (TARGETS,), 0, 4)
    noise = jax.random.normal(noise_key, (TARGETS, F), jnp.float32)
    return (noise + 0.8 * directions[picks]).astype(jnp.bfloat16)


def draw_signs(key, part):
    key = jax.random.fold_in(key, 3)
    return 2 * jax.random.randint(key, (NBLK, P_SIZE), 0, 2) - 1


def setup_inputs(seed: int = 0) -> dict:
    seeds = jax.random.split(jax.random.key(seed), 5)
    return {
        "train_grads": draw_train_grads(jax.random.fold_in(seeds[4], 71), 0),
        "target_grads": draw_target_grads(jax.random.fold_in(seeds[4], 71), 0),
        "signs": draw_signs(jax.random.fold_in(seeds[4], 71), 0),
        "block_order": jax.random.permutation(seeds[3], NBLK).astype(jnp.int32),
    }


def hadamard(values):
    length_now = values.shape[-1]
    leading = values.shape[:-1]
    half_span = 1
    while half_span < length_now:
        grouped = values.reshape(leading + (length_now // (2 * half_span), 2, half_span))
        first_half = grouped[..., 0, :]
        second_half = grouped[..., 1, :]
        values = jnp.stack([first_half + second_half, first_half - second_half], axis=-2).reshape(leading + (length_now,))
        half_span = half_span * 2
    return values

def normalize(projected):
    widened = projected.astype(jnp.float32)
    row_scale = lax.rsqrt(lax.optimization_barrier(jnp.mean(widened * widened, axis=-1, keepdims=True)) + 1e-06)
    return (widened * row_scale).astype(jnp.bfloat16)

def project(gradients, signs, block_order):
    proj_width = signs.shape[1]
    row_count = gradients.shape[0]

    def add_block(running, inputs):
        position, sign_row = inputs
        block = lax.dynamic_slice_in_dim(gradients, (position * proj_width).astype(jnp.int32), proj_width, 1)
        return (running + block.astype(jnp.float32) * sign_row.astype(jnp.float32)[None, :], None)
    summed, unused = lax.scan(add_block, jnp.zeros((row_count, proj_width), jnp.float32), (block_order, signs))
    transformed = hadamard(summed) * (1.0 / math.sqrt(F))
    return normalize(transformed.astype(jnp.bfloat16))

def reference(train_grads, target_grads, signs, block_order):
    train_features = project(train_grads, signs, block_order)
    target_normed = project(target_grads, signs, block_order)
    products = jnp.dot(train_features, target_normed.T, preferred_element_type=jnp.float32) / P_SIZE
    cosines = products.reshape(EXAMPLES, N_EX, TGT_DEV)
    return (train_features, cosines)
```

```python
import functools

import jax
import jax.numpy as jnp
from jax import lax
from jax.experimental import pallas as pl
from jax.experimental.pallas import tpu as pltpu
from jax.sharding import PartitionSpec as P

MESH = pl.DeviceIdType.MESH
BF = jnp.bfloat16
F32 = jnp.float32

W = 512
PROJ = 8192
NF = 16
NY = 4
NX = 2
U = NY + NX
TRAIN = 16 * NY + 32 * NX
NT = (((1,), (1,)), ((), ()))
FAR_FIRST = (4, 3, 5, 2, 6, 1, 7)
PAIRS = ((0, 1), (7, 2), (6, 3), (5, 4))
ROUNDS = 2
PEERS = tuple((a, d) for d in (4, 3, 5, 2, 6, 1, 7, 0) for a in (1, 0) if (a, d) != (0, 0))


def butterfly(values):
    span = 1
    while span < len(values):
        out = list(values)
        for i in range(len(values)):
            if not i & span:
                out[i] = values[i] + values[i + span]
                out[i + span] = values[i] - values[i + span]
        values = out
        span *= 2
    return values


def kernel(
    train_hbm, target_hbm, signs_hbm, order_ref,
    feat_out, cos_out,
    tr_v, tg_v, sg_v, lsig, had, perm,
    mt, rxt, rcvt, my, mx, rxx, rcv, zs, rzs, tall, proj, stat, rstat, part, rpart,
    ld, tx_s, tx_r, xx_s, xx_r, ty_s, ty_r, it_s, it_r, yx_s, yx_r, xl_s, xl_r, zz_s, zz_r, cc_s, cc_r, st_s, st_r, co_s, co_r,
):
    f = lax.axis_index("feat")
    e = lax.axis_index("ex")
    h, y = f // 8, f % 8
    z, xl, c = e // 4, (e // 2) % 2, e % 2
    oh = 1 - h

    def on_feat(a, d):
        return (((h + a) % 2) * 8 + (y + d) % 8, e)

    def on_z(d):
        return (f, ((z + d) % 8) * 4 + xl * 2 + c)

    xl_dev = (f, z * 4 + (1 - xl) * 2 + c)
    core_dev = (f, z * 4 + xl * 2 + (1 - c))

    def remote(src, dst, s, r, dev):
        return pltpu.make_async_remote_copy(
            src_ref=src, dst_ref=dst, send_sem=s, recv_sem=r, device_id=dev, device_id_type=MESH
        )

    barrier = pltpu.get_barrier_semaphore()
    partners = [on_feat(a, d) for a, d in PEERS] + [on_z(d) for d in range(1, 8)] + [xl_dev, core_dev]
    for dev in partners:
        pl.semaphore_signal(barrier, inc=1, device_id=dev, device_id_type=MESH)

    loads = [
        pltpu.make_async_copy(signs_hbm, sg_v, ld.at[0]),
        pltpu.make_async_copy(target_hbm, tg_v, ld.at[1]),
    ]
    for u in range(U):
        lo, n = (16 * u, 16) if u < NY else (16 * NY + 32 * (u - NY), 32)
        loads.append(
            pltpu.make_async_copy(train_hbm.at[pl.ds(lo, n)], tr_v.at[pl.ds(lo, n)], ld.at[2 + u])
        )
    for load in loads:
        load.start()

    parity = lax.broadcasted_iota(jnp.int32, (W, W), 0) & lax.broadcasted_iota(jnp.int32, (W, W), 1)
    for shift in (8, 4, 2, 1):
        parity = parity ^ (parity >> shift)
    had[...] = (1 - 2 * (parity & 1)).astype(F32).astype(BF)
    n_out = lax.broadcasted_iota(jnp.int32, (256, 256), 0)
    n_in = lax.broadcasted_iota(jnp.int32, (256, 256), 1)
    wanted = (
        ((n_out >> 3) & 1) * 128 + ((n_out >> 1) & 1) * 64 + ((n_out >> 2) & 1) * 32 + (n_out >> 4) * 2 + (n_out & 1)
    )
    perm[...] = jnp.where(wanted == n_in, 1.0, 0.0).astype(BF)

    loads[0].wait()
    slot = lax.broadcasted_iota(jnp.int32, (8, 32), 0)
    chosen = (order_ref[...] == f * 2 + slot) & (slot < 2)
    lsig[...] = jnp.dot(
        jnp.where(chosen, 1.0, 0.0).astype(BF),
        sg_v[...].astype(F32).astype(BF),
        preferred_element_type=F32,
    )

    def premix(grads, row, store):
        def tile(t, carry):
            values = []
            for b in range(NF):
                at0 = pl.ds(pl.multiple_of(b * W + t * 128, 128), 128)
                at1 = pl.ds(pl.multiple_of(PROJ + b * W + t * 128, 128), 128)
                g0 = grads[pl.ds(row, 16), at0].astype(F32)
                g1 = grads[pl.ds(row, 16), at1].astype(F32)
                values.append(g0 * lsig[pl.ds(0, 1), at0] + g1 * lsig[pl.ds(1, 1), at0])
            lanes = pl.ds(pl.multiple_of(t * 128, 128), 128)
            for dest, value in enumerate(butterfly(values)):
                store(dest, lanes, value.astype(BF))
            return carry

        lax.fori_loop(0, W // 128, tile, 0)

    def store_split(buf, k):
        def store(dest, lanes, value):
            buf[dest // 8, dest % 8, pl.ds(16 * k, 16), lanes] = value

        return store

    def store_y(u):
        def store(dest, lanes, value):
            my[u, dest % 8, pl.ds(16 * (dest // 8), 16), lanes] = value

        return store

    def yy(d):
        return (y + d) % 8

    tx = {d: remote(mt.at[oh, yy(d)], rxt.at[yy(d)], tx_s.at[d], tx_r.at[d], on_feat(1, 0)) for d in range(8)}
    xx = {
        (u, d): remote(mx.at[u, oh, yy(d)], rxx.at[u, yy(d)], xx_s.at[u, d], xx_r.at[u, d], on_feat(1, 0))
        for u in range(NX)
        for d in range(8)
    }
    ty = {d: remote(mt.at[h, yy(d)], rcvt.at[d - 1], ty_s.at[d - 1], ty_r.at[d - 1], on_feat(0, d)) for d in range(1, 8)}

    def own(u, d):
        return my.at[u, yy(d)] if u < NY else mx.at[u - NY, h, yy(d)]

    it = {}
    for u in range(U):
        for way, sign in ((0, 1), (1, -1)):
            for s in range(4):
                rows = pl.ds(16 * way, 16) if s == 0 else pl.ds(0, 32)
                it[u, way, s] = remote(
                    own(u, sign * (4 - s) + 8).at[rows],
                    rcv.at[u, way, s, rows],
                    it_s.at[u, way, s],
                    it_r.at[u, way, s],
                    on_feat(0, sign + 8),
                )
    yx = {u: remote(zs.at[u, oh], rzs.at[u], yx_s.at[u], yx_r.at[u], on_feat(1, 0)) for u in range(NY)}
    own_t = tall.at[0, c, xl]
    other_t = tall.at[0, c, 1 - xl]
    xlc = remote(own_t, own_t, xl_s, xl_r, xl_dev)
    zz = {}
    for d in range(1, 8):
        zz[0, d] = remote(own_t, tall.at[8 - d, c, xl], zz_s.at[0, 8 - d], zz_r.at[0, 8 - d], on_z(d))
        zz[1, d] = remote(other_t, tall.at[8 - d, c, 1 - xl], zz_s.at[1, 8 - d], zz_r.at[1, 8 - d], on_z(d))
    cc = {d: remote(tall.at[d, c], tall.at[d, c], cc_s.at[d], cc_r.at[d], core_dev) for d in range(8)}
    st = {
        j: remote(stat, rstat.at[j], st_s.at[j], st_r.at[j], on_feat(a, d)) for j, (a, d) in enumerate(PEERS)
    }
    co = {}
    for r in range(ROUNDS):
        rows = pl.ds(32 * r, 32 if r + 1 < ROUNDS else 48)
        for j, (a, d) in enumerate(PEERS):
            dev = on_feat(a, d)
            co[r, j] = remote(part.at[dev[0], rows], rpart.at[j, rows], co_s.at[r, j], co_r.at[r, j], dev)

    sent = []

    def start(copy):
        copy.start()
        sent.append(copy)

    def add(to, rows, arrived):
        to[rows] = (to[rows].astype(F32) + arrived.astype(F32)).astype(BF)

    every = pl.ds(0, 32)

    def step(u, s):
        for way, sign in ((0, 1), (1, -1)):
            to = own(u, sign * (4 - s) + 8)
            if u >= NY:
                xu = u - NY
                d = (sign * (4 - s) + 8) % 8
                if s > 0 or way == 0:
                    xx[xu, d].wait_recv()
                    add(to, every, rxx[xu, yy(d)])
            if s > 0:
                it[u, way, s - 1].wait_recv()
                rows = pl.ds(16 * way, 16) if s == 1 else every
                add(to, rows, rcv[u, way, s - 1, rows])
            start(it[u, way, s])

    def transform(rows_sum, row, n):
        high = rows_sum.astype(BF)
        low = (rows_sum - high.astype(F32)).astype(BF)
        table = had[...]
        done = jnp.dot(high, table, preferred_element_type=F32) + jnp.dot(low, table, preferred_element_type=F32)
        return (done * (2.0**-9)).astype(BF)

    def gather_step(u):
        if u >= NY:
            xx[u - NY, 0].wait_recv()
        it[u, 0, 3].wait_recv()
        it[u, 1, 3].wait_recv()
        total = own(u, 0)[...].astype(F32) + rcv[u, 0, 3].astype(F32) + rcv[u, 1, 3].astype(F32)
        if u >= NY:
            return total + rxx[u - NY, yy(0)].astype(F32)
        return total

    def finish_y_send(u):
        total = gather_step(u)
        zs[u] = total.reshape(2, 16, W).astype(BF)
        start(yx[u])

    def finish_y(u):
        yx[u].wait_recv()
        total = zs[u, h].astype(F32) + rzs[u].astype(F32)
        proj[pl.ds(16 * u, 16)] = transform(total, 16 * u, 16)

    def finish_x(u):
        row = 16 * NY + 32 * (u - NY)
        proj[pl.ds(row, 32)] = transform(gather_step(u), row, 32)

    def target_step(d):
        tx[d].wait_recv()
        add(mt.at[h, yy(d)], every, rxt[yy(d)])
        start(ty[d])

    def target_finish():
        tx[0].wait_recv()
        total = mt[h, y].astype(F32) + rxt[yy(0)].astype(F32)
        for d in FAR_FIRST:
            ty[d].wait_recv()
            total = total + rcvt[d - 1].astype(F32)
        tall[0, c, xl] = transform(total, 0, 32)
        start(xlc)
        for d in FAR_FIRST:
            start(zz[0, d])

    def target_second():
        xlc.wait_recv()
        for d in FAR_FIRST:
            start(zz[1, d])
        start(cc[0])

    def forward(d):
        zz[0, 8 - d].wait_recv()
        zz[1, 8 - d].wait_recv()
        start(cc[d])

    loads[1].wait()
    for k in range(2):
        premix(tg_v, 16 * k, store_split(mt, k))
    pl.semaphore_wait(barrier, len(partners))
    for d in FAR_FIRST + (0,):
        start(tx[d])
    for u in range(NY):
        loads[2 + u].wait()
        premix(tr_v, 16 * u, store_y(u))
        step(u, 0)
    for u in range(NX):
        loads[2 + NY + u].wait()
        for k in range(2):
            premix(tr_v, 16 * NY + 32 * u + 16 * k, store_split(mx.at[u], k))
    for d in FAR_FIRST + (0,):
        for u in range(NX):
            start(xx[u, d])

    queue = list(FAR_FIRST)
    for u in range(NY):
        target_step(queue.pop(0))
        step(u, 1)
    for d in queue:
        target_step(d)
    for u in range(NY):
        step(u, 2)
    for u in range(NX):
        step(NY + u, 0)
    target_finish()
    for u in range(NY):
        step(u, 3)
    for u in range(NX):
        step(NY + u, 1)
    target_second()
    for u in range(NX):
        step(NY + u, 2)
    for u in range(NY):
        finish_y_send(u)
    for u in range(NX):
        step(NY + u, 3)
    for u in range(NY):
        finish_y(u)
    for u in range(NX):
        finish_x(NY + u)

    wide = proj[...].astype(F32)
    square = wide * wide
    high = square.astype(BF)
    low = (square - high.astype(F32)).astype(BF)
    ones = jnp.ones((8, W), BF)
    stat[...] = lax.dot_general(ones, high, NT, preferred_element_type=F32) + lax.dot_general(
        ones, low, NT, preferred_element_type=F32
    )
    for j in range(len(PEERS)):
        start(st[j])
    for pair in PAIRS[:2]:
        for d in pair:
            if d:
                forward(d)
    total = stat[...]
    for j in range(len(PEERS)):
        st[j].wait_recv()
        total = total + rstat[j]
    scale = lax.rsqrt(total[0:1] * (1.0 / PROJ) + 1e-06)
    eye = lax.broadcasted_iota(jnp.int32, (TRAIN, TRAIN), 0) == lax.broadcasted_iota(jnp.int32, (TRAIN, TRAIN), 1)
    column = jnp.sum(jnp.where(eye, scale, 0.0), axis=1, keepdims=True)
    proj[...] = (proj[...].astype(F32) * column).astype(BF)
    feat_out[...] = proj[...]

    lane = lax.broadcasted_iota(jnp.int32, (256, 128), 1)
    squares = jnp.zeros((256, 128), F32)
    for k, pair in enumerate(PAIRS):
        if k >= 2:
            for d in pair:
                forward(d)
        for d in pair:
            cc[d].wait_recv()
        rows = jnp.concatenate([tall[d].reshape(128, W) for d in pair], axis=0)
        products = lax.dot_general(rows, proj[...], NT, preferred_element_type=F32).astype(BF)
        ordered = jnp.dot(perm[...], products, preferred_element_type=F32).astype(BF)
        part[:, pl.ds(16 * k, 16), :] = ordered.reshape(NF, 16, TRAIN)
        wide = rows.astype(F32)
        norm = jnp.sum(wide * wide, axis=1, keepdims=True)
        norm_high = norm.astype(BF).astype(F32)
        squares = squares + jnp.where(lane == 2 * k, norm_high, 0.0) + jnp.where(lane == 2 * k + 1, norm - norm_high, 0.0)
        if k == len(PAIRS) - 1:
            moved = jnp.dot(perm[...], squares.astype(BF), preferred_element_type=F32).astype(BF)
            part[:, pl.ds(64, 16), :] = moved.reshape(NF, 16, 128)
        if k % 2 == 1:
            for j in range(len(PEERS)):
                start(co[k // 2, j])

    total = part[f].astype(F32)
    for j in range(len(PEERS)):
        for r in range(ROUNDS):
            co[r, j].wait_recv()
        total = total + rpart[j].astype(F32)
    lane16 = lax.broadcasted_iota(jnp.int32, (16, 128), 1)
    for k, pair in enumerate(PAIRS):
        norm = jnp.sum(jnp.where(lane16 // 2 == k, total[64:80], 0.0), axis=1, keepdims=True)
        factor = lax.rsqrt(norm * (1.0 / PROJ) + 1e-06) * (1.0 / PROJ)
        block = total[16 * k : 16 * k + 16] * factor
        for i, d in enumerate(pair):
            cos_out[pl.ds(pl.multiple_of(((z + d) % 8) * 8, 8), 8), :] = block[8 * i : 8 * i + 8]

    for copy in sent:
        copy.wait_send()


def solution(mesh):
    vm = pltpu.VMEM
    dma = pltpu.SemaphoreType.DMA
    n_peers = len(PEERS)
    scratch = [
        vm((TRAIN, 2 * PROJ), BF), vm((32, 2 * PROJ), BF), vm((32, PROJ), jnp.int32), vm((8, PROJ), F32),
        vm((W, W), BF), vm((256, 256), BF),
        vm((2, 8, 32, W), BF), vm((8, 32, W), BF), vm((7, 32, W), BF),
        vm((NY, 8, 32, W), BF), vm((NX, 2, 8, 32, W), BF), vm((NX, 8, 32, W), BF), vm((U, 2, 4, 32, W), BF),
        vm((NY, 2, 16, W), BF), vm((NY, 16, W), BF),
        vm((8, 2, 2, 32, W), BF), vm((TRAIN, W), BF),
        vm((8, 128), F32), vm((n_peers, 8, 128), F32),
        vm((NF, 80, 128), BF), vm((n_peers, 80, 128), BF),
        dma((2 + U,)), dma((8,)), dma((8,)), dma((NX, 8)), dma((NX, 8)), dma((7,)), dma((7,)),
        dma((U, 2, 4)), dma((U, 2, 4)), dma((NY,)), dma((NY,)), dma, dma, dma((2, 8)), dma((2, 8)),
        dma((8,)), dma((8,)), dma((n_peers,)), dma((n_peers,)), dma((ROUNDS, n_peers)), dma((ROUNDS, n_peers)),
    ]
    hbm = pl.BlockSpec(memory_space=pl.ANY)
    whole = pl.BlockSpec(memory_space=pltpu.VMEM)

    def local(train_grads, target_grads, signs, block_order):
        features, cosines = pl.pallas_call(
            kernel,
            out_shape=(
                jax.ShapeDtypeStruct((TRAIN, W), BF),
                jax.ShapeDtypeStruct((64, 128), F32),
            ),
            in_specs=[hbm, hbm, hbm, whole],
            out_specs=(whole, whole),
            scratch_shapes=scratch,
            compiler_params=pltpu.CompilerParams(
                collective_id=0, has_side_effects=True, vmem_limit_bytes=48 * 2**20
            ),
        )(train_grads, target_grads, signs, block_order.reshape(1, 32))
        return features, cosines.reshape(32, 2, TRAIN).transpose(2, 0, 1)

    placed = (P("ex", "feat"), P("ex", "feat"), P(), P())
    return jax.shard_map(
        local,
        mesh=mesh,
        in_specs=placed,
        out_specs=(P("ex", "feat"), P("ex", None, "feat")),
        check_vma=False,
    )
```

```python
import functools

import jax
import jax.numpy as jnp
from jax import lax
from jax.experimental import pallas as pl
from jax.experimental.pallas import tpu as pltpu
from jax.sharding import PartitionSpec as P

MESH = pl.DeviceIdType.MESH
BF = jnp.bfloat16
F32 = jnp.float32

W = 512
PROJ = 8192
VML = 53.4
NF = 16
NY = 4
NX = 2
U = NY + NX
TRAIN = 16 * NY + 32 * NX
NT = (((1,), (1,)), ((), ()))
FAR_FIRST = (4, 3, 5, 2, 6, 1, 7)
PAIRS = ((0, 4), (3, 5), (2, 6), (1, 7))
GROUPS = ((0, 1, 2), (3,))
ROUNDS = len(GROUPS)
PEERS = tuple((a, d) for d in (4, 3, 5, 2, 6, 1, 7, 0) for a in (1, 0) if (a, d) != (0, 0))


def butterfly(values):
    span = 1
    while span < len(values):
        out = list(values)
        for i in range(len(values)):
            if not i & span:
                out[i] = values[i] + values[i + span]
                out[i + span] = values[i] - values[i + span]
        values = out
        span *= 2
    return values


def kernel(
    train_hbm, target_hbm, signs_hbm, order_ref,
    feat_out, cos_out,
    tr_v, tg_v, sg_v, lsig, had, perm,
    mt, rt4, rt, zt, rzt, my, mx, rxx, rcv, zs, rzs, tall, proj, stat, rstat, part, rpart,
    ld, xx_s, xx_r, ty_s, ty_r, it_s, it_r, yx_s, yx_r, tq_s, tq_r, zz_s, zz_r, cc_s, cc_r, st_s, st_r, co_s, co_r, far_z,
):
    f = lax.axis_index("feat")
    e = lax.axis_index("ex")
    h, y = f // 8, f % 8
    z, xl, c = e // 4, (e // 2) % 2, e % 2
    oh = 1 - h

    def on_feat(a, d):
        return (((h + a) % 2) * 8 + (y + d) % 8, e)

    def on_z(d):
        return (f, ((z + d) % 8) * 4 + xl * 2 + c)

    across = [(f, z * 4 + (1 - xl) * 2 + c), on_feat(1, 0), (oh * 8 + y, z * 4 + (1 - xl) * 2 + c)]
    core_dev = (f, z * 4 + xl * 2 + (1 - c))

    def remote(src, dst, s, r, dev):
        return pltpu.make_async_remote_copy(
            src_ref=src, dst_ref=dst, send_sem=s, recv_sem=r, device_id=dev, device_id_type=MESH
        )

    loads = [
        pltpu.make_async_copy(signs_hbm, sg_v, ld.at[0]),
        pltpu.make_async_copy(target_hbm.at[pl.ds(0, 16)], tg_v.at[pl.ds(0, 16)], ld.at[1]),
        pltpu.make_async_copy(target_hbm.at[pl.ds(16, 16)], tg_v.at[pl.ds(16, 16)], ld.at[2]),
    ]
    for u in range(U):
        lo, n = (16 * u, 16) if u < NY else (16 * NY + 32 * (u - NY), 32)
        loads.append(
            pltpu.make_async_copy(train_hbm.at[pl.ds(lo, n)], tr_v.at[pl.ds(lo, n)], ld.at[3 + u])
        )
    for load in loads[:3]:
        load.start()

    barrier = pltpu.get_barrier_semaphore()
    partners = [on_feat(0, d) for d in (2, 6, 1, 7)] + across + [on_z(d) for d in (2, 6, 1, 7)] + [core_dev]
    for dev in partners:
        pl.semaphore_signal(barrier, inc=1, device_id=dev, device_id_type=MESH)

    loads[0].wait()
    slot = lax.broadcasted_iota(jnp.int32, (8, 32), 0)
    chosen = (order_ref[...] == f * 2 + slot) & (slot < 2)
    lsig[...] = jnp.dot(
        jnp.where(chosen, 1.0, 0.0).astype(BF),
        sg_v[...].astype(F32).astype(BF),
        preferred_element_type=F32,
    )

    def tables():
        parity = lax.broadcasted_iota(jnp.int32, (W, W), 0) & lax.broadcasted_iota(jnp.int32, (W, W), 1)
        for shift in (8, 4, 2, 1):
            parity = parity ^ (parity >> shift)
        had[...] = (1 - 2 * (parity & 1)).astype(F32).astype(BF)
        n_out = lax.broadcasted_iota(jnp.int32, (256, 256), 0)
        n_in = lax.broadcasted_iota(jnp.int32, (256, 256), 1)
        wanted = (
            ((n_out >> 3) & 1) * 128
            + ((n_out >> 1) & 1) * 64
            + (n_out >> 7) * 32
            + ((n_out >> 2) & 1) * 16
            + ((n_out >> 4) & 7) * 2
            + (n_out & 1)
        )
        perm[...] = jnp.where(wanted == n_in, 1.0, 0.0).astype(BF)

    def premix(grads, row, store):
        def tile(t, carry):
            values = []
            for b in range(NF):
                at0 = pl.ds(pl.multiple_of(b * W + t * 128, 128), 128)
                at1 = pl.ds(pl.multiple_of(PROJ + b * W + t * 128, 128), 128)
                g0 = grads[pl.ds(row, 16), at0].astype(F32)
                g1 = grads[pl.ds(row, 16), at1].astype(F32)
                values.append(g0 * lsig[pl.ds(0, 1), at0] + g1 * lsig[pl.ds(1, 1), at0])
            lanes = pl.ds(pl.multiple_of(t * 128, 128), 128)
            for dest, value in enumerate(butterfly(values)):
                store(dest, lanes, value.astype(BF))
            return carry

        lax.fori_loop(0, W // 128, tile, 0)

    def store_split(buf, k):
        def store(dest, lanes, value):
            buf[dest // 8, dest % 8, pl.ds(16 * k, 16), lanes] = value

        return store

    def store_y(buf):
        def store(dest, lanes, value):
            buf[dest % 8, pl.ds(16 * (dest // 8), 16), lanes] = value

        return store

    def yy(d):
        return (y + d) % 8

    xx = {
        (u, d): remote(mx.at[u, oh, yy(d)], rxx.at[u, yy(d)], xx_s.at[u, d], xx_r.at[u, d], on_feat(1, 0))
        for u in range(NX)
        for d in range(8)
    }
    ty = {}
    for k in range(2):
        for way, sign in ((0, 1), (1, -1)):
            rows = pl.ds(16 * way, 16)
            for name, apart, hops in ((3, 3, 1), (1, 1, 1), (2, 2, 2)):
                ty[k, way, name] = remote(
                    mt.at[k, yy(8 + sign * apart)], rt.at[k, way, name - 1],
                    ty_s.at[k, way, name - 1], ty_r.at[k, way, name - 1], on_feat(0, 8 + sign * hops),
                )
            ty[k, way, 4] = remote(
                mt.at[k, yy(4), rows], rt4.at[k, way], ty_s.at[k, way, 3], ty_r.at[k, way, 3], on_feat(0, 8 + 2 * sign)
            )
    tq = {
        (k, i): remote(zt.at[k, h if i == 0 else oh], rzt.at[k, i], tq_s.at[k, i], tq_r.at[k, i], across[i])
        for k in range(2)
        for i in range(3)
    }

    def own(u, d):
        return my.at[u, yy(d)] if u < NY else mx.at[u - NY, h, yy(d)]

    it = {}
    for u in range(U):
        for way, sign in ((0, 1), (1, -1)):
            for s in range(4):
                rows = pl.ds(16 * way, 16) if s == 0 else pl.ds(0, 32)
                it[u, way, s] = remote(
                    own(u, sign * (4 - s) + 8).at[rows],
                    rcv.at[u, way, s, rows],
                    it_s.at[u, way, s],
                    it_r.at[u, way, s],
                    on_feat(0, sign + 8),
                )
    yx = {u: remote(zs.at[u, oh], rzs.at[u], yx_s.at[u], yx_r.at[u], on_feat(1, 0)) for u in range(NY)}
    zz = {
        (k, d): remote(
            tall.at[0, c, k], tall.at[8 - d, c, k], zz_s.at[k, 8 - d], zz_r.at[k, 8 - d], on_z(d)
        )
        for k in range(2)
        for d in range(1, 8)
    }
    cc = {d: remote(tall.at[d, c], tall.at[d, c], cc_s.at[d], cc_r.at[d], core_dev) for d in range(8)}
    st = {
        j: remote(stat, rstat.at[j], st_s.at[j], st_r.at[j], on_feat(a, d)) for j, (a, d) in enumerate(PEERS)
    }
    co = {}
    for r in range(ROUNDS):
        rows = pl.ds(16 * GROUPS[r][0], 16 * len(GROUPS[r]) + (0 if r + 1 < ROUNDS else 16))
        for j, (a, d) in enumerate(PEERS):
            dev = on_feat(a, d)
            co[r, j] = remote(part.at[dev[0], rows], rpart.at[j, rows], co_s.at[r, j], co_r.at[r, j], dev)

    sent = []

    def start(copy):
        copy.start()
        sent.append(copy)

    def add(to, rows, arrived):
        to[rows] = (to[rows].astype(F32) + arrived.astype(F32)).astype(BF)

    every = pl.ds(0, 32)

    def step(u, s):
        for way, sign in ((0, 1), (1, -1)):
            to = own(u, sign * (4 - s) + 8)
            if u >= NY:
                xu = u - NY
                d = (sign * (4 - s) + 8) % 8
                if s > 0 or way == 0:
                    xx[xu, d].wait_recv()
                    add(to, every, rxx[xu, yy(d)])
            if s > 0:
                it[u, way, s - 1].wait_recv()
                rows = pl.ds(16 * way, 16) if s == 1 else every
                add(to, rows, rcv[u, way, s - 1, rows])
            start(it[u, way, s])

    def transform(rows_sum):
        high = rows_sum.astype(BF)
        low = (rows_sum - high.astype(F32)).astype(BF)
        table = had[...]
        done = jnp.dot(high, table, preferred_element_type=F32) + jnp.dot(low, table, preferred_element_type=F32)
        return (done * (2.0**-9)).astype(BF)

    def gather_step(u):
        if u >= NY:
            xx[u - NY, 0].wait_recv()
        it[u, 0, 3].wait_recv()
        it[u, 1, 3].wait_recv()
        total = own(u, 0)[...].astype(F32) + rcv[u, 0, 3].astype(F32) + rcv[u, 1, 3].astype(F32)
        if u >= NY:
            return total + rxx[u - NY, yy(0)].astype(F32)
        return total

    def finish_y_send(u):
        total = gather_step(u)
        zs[u] = total.reshape(2, 16, W).astype(BF)
        start(yx[u])

    def finish_y(u):
        yx[u].wait_recv()
        total = zs[u, h].astype(F32) + rzs[u].astype(F32)
        proj[pl.ds(16 * u, 16)] = transform(total)

    def finish_x(u):
        row = 16 * NY + 32 * (u - NY)
        proj[pl.ds(row, 32)] = transform(gather_step(u))

    def target_one(k):
        for name in (4, 3, 1):
            for way in range(2):
                start(ty[k, way, name])

    def target_two(k):
        for way, sign in ((0, 1), (1, -1)):
            to = mt.at[k, yy(8 + 2 * sign)]
            ty[k, way, 3].wait_recv()
            ty[k, way, 4].wait_recv()
            add(to, every, rt[k, way, 2])
            add(to, pl.ds(16 * way, 16), rt4[k, way])
            start(ty[k, way, 2])

    def target_across(k):
        total = mt[k, y].astype(F32)
        for name in (1, 2):
            for way in range(2):
                ty[k, way, name].wait_recv()
                total = total + rt[k, way, name - 1].astype(F32)
        zt[k] = total.reshape(2, 16, W).astype(BF)
        for i in (1, 2, 0):
            start(tq[k, i])

    def target_finish(k):
        for i in range(3):
            tq[k, i].wait_recv()
        mine = zt[k, h].astype(F32) + rzt[k, 1].astype(F32)
        other = rzt[k, 0].astype(F32) + rzt[k, 2].astype(F32)
        done = transform(jnp.concatenate([mine, other], axis=0))
        tall[0, c, k, xl] = done[0:16]
        tall[0, c, k, 1 - xl] = done[16:32]
        for d in FAR_FIRST:
            start(zz[k, d])

    def send_x(u, distances):
        for d in distances:
            start(xx[u, d])

    def forward(d):
        zz[0, 8 - d].wait_recv()
        zz[1, 8 - d].wait_recv()
        start(cc[d])

    loads[1].wait()
    for load in loads[3:]:
        load.start()
    premix(tg_v, 0, store_y(mt.at[0]))
    pl.semaphore_wait(barrier, len(partners))
    target_one(0)
    for d in (2, 6):
        pl.semaphore_signal(far_z, inc=1, device_id=on_z(d), device_id_type=MESH)
    loads[2].wait()
    premix(tg_v, 16, store_y(mt.at[1]))
    target_one(1)
    for u in range(NY):
        loads[3 + u].wait()
        premix(tr_v, 16 * u, store_y(my.at[u]))
        step(u, 0)
    for u in range(NX):
        loads[3 + NY + u].wait()
        for k in range(2):
            premix(tr_v, 16 * NY + 32 * u + 16 * k, store_split(mx.at[u], k))
    send_x(0, FAR_FIRST + (0,))
    send_x(1, FAR_FIRST[:1])
    target_two(0)
    target_two(1)
    tables()
    for u in range(2):
        step(u, 1)
    target_across(0)
    for u in range(2, NY):
        step(u, 1)
    target_across(1)
    send_x(1, FAR_FIRST[1:] + (0,))
    for u in range(NX):
        step(NY + u, 0)
    for u in range(2):
        step(u, 2)
    pl.semaphore_wait(far_z, 2)
    target_finish(0)
    for u in range(2, NY):
        step(u, 2)
    target_finish(1)
    start(cc[0])
    for u in range(NX):
        step(NY + u, 1)
    for u in range(NY):
        step(u, 3)
    for u in range(NX):
        step(NY + u, 2)
    for u in range(NY):
        finish_y_send(u)
    for u in range(NX):
        step(NY + u, 3)
    for u in range(NY):
        finish_y(u)
    for u in range(NX):
        finish_x(NY + u)

    wide = proj[...].astype(F32)
    square = wide * wide
    high = square.astype(BF)
    low = (square - high.astype(F32)).astype(BF)
    ones = jnp.ones((8, W), BF)
    stat[...] = lax.dot_general(ones, high, NT, preferred_element_type=F32) + lax.dot_general(
        ones, low, NT, preferred_element_type=F32
    )
    for j in range(len(PEERS)):
        start(st[j])
    local = jnp.sum(square, axis=1, keepdims=True)
    scaled_t = (wide * lax.rsqrt(local * (1.0 / W) + 1e-30)).astype(BF).T
    for d in FAR_FIRST:
        forward(d)

    lane = lax.broadcasted_iota(jnp.int32, (256, 128), 1)
    squares = jnp.zeros((256, 128), F32)
    for k, pair in enumerate(PAIRS):
        for d in pair:
            cc[d].wait_recv()
        rows = jnp.concatenate([tall[d].reshape(128, W) for d in pair], axis=0)
        products = jnp.dot(rows, scaled_t, preferred_element_type=F32).astype(BF)
        ordered = jnp.dot(perm[...], products, preferred_element_type=F32).astype(BF)
        part[:, pl.ds(16 * k, 16), :] = ordered.reshape(NF, 16, TRAIN)
        wide = rows.astype(F32)
        norm = jnp.sum(wide * wide, axis=1, keepdims=True)
        norm_high = norm.astype(BF).astype(F32)
        squares = squares + jnp.where(lane == 2 * k, norm_high, 0.0) + jnp.where(lane == 2 * k + 1, norm - norm_high, 0.0)
        if k == len(PAIRS) - 1:
            moved = jnp.dot(perm[...], squares.astype(BF), preferred_element_type=F32).astype(BF)
            part[:, pl.ds(64, 16), :] = moved.reshape(NF, 16, 128)
        for r in range(ROUNDS):
            if GROUPS[r][-1] == k:
                for j in range(len(PEERS)):
                    start(co[r, j])

    sums = stat[...]
    for j in range(len(PEERS)):
        st[j].wait_recv()
        sums = sums + rstat[j]
    scale = lax.rsqrt(sums[0:1] * (1.0 / PROJ) + 1e-06)
    eye = lax.broadcasted_iota(jnp.int32, (TRAIN, TRAIN), 0) == lax.broadcasted_iota(jnp.int32, (TRAIN, TRAIN), 1)
    column = jnp.sum(jnp.where(eye, scale, 0.0), axis=1, keepdims=True)
    feat_out[...] = (proj[...].astype(F32) * column).astype(BF)

    def undo(sums):
        mean = sums[0:1] * (1.0 / W) + 1e-30
        return mean * lax.rsqrt(mean) * scale

    moved_sum = part[f, pl.ds(64, 16)].astype(F32)
    total = part[f, pl.ds(0, 64)].astype(F32) * undo(stat)
    for j in range(len(PEERS)):
        for r in range(ROUNDS):
            co[r, j].wait_recv()
        moved_sum = moved_sum + rpart[j, pl.ds(64, 16)].astype(F32)
        total = total + rpart[j, pl.ds(0, 64)].astype(F32) * undo(rstat[j])
    lane16 = lax.broadcasted_iota(jnp.int32, (16, 128), 1)
    for k, pair in enumerate(PAIRS):
        norm = jnp.sum(jnp.where(lane16 // 2 == k, moved_sum, 0.0), axis=1, keepdims=True)
        factor = lax.rsqrt(norm * (1.0 / PROJ) + 1e-06) * (1.0 / PROJ)
        block = total[16 * k : 16 * k + 16] * factor
        for i, d in enumerate(pair):
            cos_out[pl.ds(pl.multiple_of(((z + d) % 8) * 8, 8), 8), :] = block[8 * i : 8 * i + 8]

    for copy in sent:
        copy.wait_send()


def solution(mesh):
    vm = pltpu.VMEM
    dma = pltpu.SemaphoreType.DMA
    n_peers = len(PEERS)
    scratch = [
        vm((TRAIN, 2 * PROJ), BF), vm((32, 2 * PROJ), BF), vm((32, PROJ), jnp.int32), vm((8, PROJ), F32),
        vm((W, W), BF), vm((256, 256), BF),
        vm((2, 8, 32, W), BF), vm((2, 2, 16, W), BF), vm((2, 2, 3, 32, W), BF), vm((2, 2, 16, W), BF), vm((2, 3, 16, W), BF),
        vm((NY, 8, 32, W), BF), vm((NX, 2, 8, 32, W), BF), vm((NX, 8, 32, W), BF), vm((U, 2, 4, 32, W), BF),
        vm((NY, 2, 16, W), BF), vm((NY, 16, W), BF),
        vm((8, 2, 2, 2, 16, W), BF), vm((TRAIN, W), BF),
        vm((8, 128), F32), vm((n_peers, 8, 128), F32),
        vm((NF, 80, 128), BF), vm((n_peers, 80, 128), BF),
        dma((3 + U,)), dma((NX, 8)), dma((NX, 8)), dma((2, 2, 4)), dma((2, 2, 4)),
        dma((U, 2, 4)), dma((U, 2, 4)), dma((NY,)), dma((NY,)), dma((2, 3)), dma((2, 3)), dma((2, 8)), dma((2, 8)),
        dma((8,)), dma((8,)), dma((n_peers,)), dma((n_peers,)), dma((ROUNDS, n_peers)), dma((ROUNDS, n_peers)),
        pltpu.SemaphoreType.REGULAR,
    ]
    hbm = pl.BlockSpec(memory_space=pl.ANY)
    whole = pl.BlockSpec(memory_space=pltpu.VMEM)

    def local(train_grads, target_grads, signs, block_order):
        features, cosines = pl.pallas_call(
            kernel,
            out_shape=(
                jax.ShapeDtypeStruct((TRAIN, W), BF),
                jax.ShapeDtypeStruct((64, 128), F32),
            ),
            in_specs=[hbm, hbm, hbm, whole],
            out_specs=(whole, whole),
            scratch_shapes=scratch,
            compiler_params=pltpu.CompilerParams(
                collective_id=0, has_side_effects=True, vmem_limit_bytes=int(VML * 2**20)
            ),
        )(train_grads, target_grads, signs, block_order.reshape(1, 32))
        return features, cosines.reshape(32, 2, TRAIN).transpose(2, 0, 1)

    placed = (P("ex", "feat"), P("ex", "feat"), P(), P())
    return jax.shard_map(
        local,
        mesh=mesh,
        in_specs=placed,
        out_specs=(P("ex", "feat"), P("ex", None, "feat")),
        check_vma=False,
    )
```

```python
import functools

import jax
import jax.numpy as jnp
from jax import lax
from jax.experimental import pallas as pl
from jax.experimental.pallas import tpu as pltpu
from jax.sharding import PartitionSpec as P

MESH = pl.DeviceIdType.MESH
BF = jnp.bfloat16
F32 = jnp.float32

W = 512
PROJ = 8192
VML = 53.4
NF = 16
NY = 4
NX = 2
U = NY + NX
TRAIN = 16 * NY + 32 * NX
NT = (((1,), (1,)), ((), ()))
FAR_FIRST = (4, 3, 5, 2, 6, 1, 7)
PAIRS = ((0, 4), (3, 5), (2, 6), (1, 7))
PEERS = tuple((a, d) for d in (4, 3, 5, 2, 6, 1, 7, 0) for a in (1, 0) if (a, d) != (0, 0))


def butterfly(values):
    span = 1
    while span < len(values):
        out = list(values)
        for i in range(len(values)):
            if not i & span:
                out[i] = values[i] + values[i + span]
                out[i + span] = values[i] - values[i + span]
        values = out
        span *= 2
    return values


def kernel(
    train_hbm, target_hbm, signs_hbm, order_ref,
    feat_out, cos_out,
    tr_v, tg_v, sg_v, lsig, had, perm,
    mt, rt4, rt, zt, rzt, my, mx, rxx, rcv, zs, rzs, tall, proj, stat, rstat, part, rpart, norms, rnorms,
    ld, xx_s, xx_r, ty_s, ty_r, it_s, it_r, yx_s, yx_r, tq_s, tq_r, zz_s, zz_r, cc_s, cc_r, st_s, st_r, co_s, co_r, ct_s, ct_r, far_z,
):
    f = lax.axis_index("feat")
    e = lax.axis_index("ex")
    h, y = f // 8, f % 8
    z, xl, c = e // 4, (e // 2) % 2, e % 2
    oh = 1 - h

    def on_feat(a, d):
        return (((h + a) % 2) * 8 + (y + d) % 8, e)

    def on_z(d):
        return (f, ((z + d) % 8) * 4 + xl * 2 + c)

    across = [(f, z * 4 + (1 - xl) * 2 + c), on_feat(1, 0), (oh * 8 + y, z * 4 + (1 - xl) * 2 + c)]
    core_dev = (f, z * 4 + xl * 2 + (1 - c))

    def remote(src, dst, s, r, dev):
        return pltpu.make_async_remote_copy(
            src_ref=src, dst_ref=dst, send_sem=s, recv_sem=r, device_id=dev, device_id_type=MESH
        )

    loads = [
        pltpu.make_async_copy(signs_hbm, sg_v, ld.at[0]),
        pltpu.make_async_copy(target_hbm.at[pl.ds(0, 16)], tg_v.at[pl.ds(0, 16)], ld.at[1]),
        pltpu.make_async_copy(target_hbm.at[pl.ds(16, 16)], tg_v.at[pl.ds(16, 16)], ld.at[2]),
    ]
    for u in range(U):
        lo, n = (16 * u, 16) if u < NY else (16 * NY + 32 * (u - NY), 32)
        loads.append(
            pltpu.make_async_copy(train_hbm.at[pl.ds(lo, n)], tr_v.at[pl.ds(lo, n)], ld.at[3 + u])
        )
    for load in loads[:3]:
        load.start()

    barrier = pltpu.get_barrier_semaphore()
    partners = [on_feat(0, d) for d in (2, 6, 1, 7)] + across + [on_z(d) for d in (2, 6, 1, 7)] + [core_dev]
    for dev in partners:
        pl.semaphore_signal(barrier, inc=1, device_id=dev, device_id_type=MESH)

    loads[0].wait()
    slot = lax.broadcasted_iota(jnp.int32, (8, 32), 0)
    chosen = (order_ref[...] == f * 2 + slot) & (slot < 2)
    lsig[...] = jnp.dot(
        jnp.where(chosen, 1.0, 0.0).astype(BF),
        sg_v[...].astype(F32).astype(BF),
        preferred_element_type=F32,
    )

    def tables():
        parity = lax.broadcasted_iota(jnp.int32, (W, W), 0) & lax.broadcasted_iota(jnp.int32, (W, W), 1)
        for shift in (8, 4, 2, 1):
            parity = parity ^ (parity >> shift)
        had[...] = (1 - 2 * (parity & 1)).astype(F32).astype(BF)
        n_out = lax.broadcasted_iota(jnp.int32, (256, 256), 0)
        n_in = lax.broadcasted_iota(jnp.int32, (256, 256), 1)
        wanted = (
            ((n_out >> 3) & 1) * 128
            + ((n_out >> 1) & 1) * 64
            + (n_out >> 7) * 32
            + ((n_out >> 2) & 1) * 16
            + ((n_out >> 4) & 7) * 2
            + (n_out & 1)
        )
        perm[...] = jnp.where(wanted == n_in, 1.0, 0.0).astype(BF)

    def premix(grads, row, store):
        def tile(t, carry):
            values = []
            for b in range(NF):
                at0 = pl.ds(pl.multiple_of(b * W + t * 128, 128), 128)
                at1 = pl.ds(pl.multiple_of(PROJ + b * W + t * 128, 128), 128)
                g0 = grads[pl.ds(row, 16), at0].astype(F32)
                g1 = grads[pl.ds(row, 16), at1].astype(F32)
                values.append(g0 * lsig[pl.ds(0, 1), at0] + g1 * lsig[pl.ds(1, 1), at0])
            lanes = pl.ds(pl.multiple_of(t * 128, 128), 128)
            for dest, value in enumerate(butterfly(values)):
                store(dest, lanes, value.astype(BF))
            return carry

        lax.fori_loop(0, W // 128, tile, 0)

    def store_split(buf, k):
        def store(dest, lanes, value):
            buf[dest // 8, dest % 8, pl.ds(16 * k, 16), lanes] = value

        return store

    def store_y(buf):
        def store(dest, lanes, value):
            buf[dest % 8, pl.ds(16 * (dest // 8), 16), lanes] = value

        return store

    def yy(d):
        return (y + d) % 8

    xx = {
        (u, d): remote(mx.at[u, oh, yy(d)], rxx.at[u, yy(d)], xx_s.at[u, d], xx_r.at[u, d], on_feat(1, 0))
        for u in range(NX)
        for d in range(8)
    }
    ty = {}
    for k in range(2):
        for way, sign in ((0, 1), (1, -1)):
            rows = pl.ds(16 * way, 16)
            for name, apart, hops in ((3, 3, 1), (1, 1, 1), (2, 2, 2)):
                ty[k, way, name] = remote(
                    mt.at[k, yy(8 + sign * apart)], rt.at[k, way, name - 1],
                    ty_s.at[k, way, name - 1], ty_r.at[k, way, name - 1], on_feat(0, 8 + sign * hops),
                )
            ty[k, way, 4] = remote(
                mt.at[k, yy(4), rows], rt4.at[k, way], ty_s.at[k, way, 3], ty_r.at[k, way, 3], on_feat(0, 8 + 2 * sign)
            )
    tq = {
        (k, i): remote(zt.at[k, h if i == 0 else oh], rzt.at[k, i], tq_s.at[k, i], tq_r.at[k, i], across[i])
        for k in range(2)
        for i in range(3)
    }

    def own(u, d):
        return my.at[u, yy(d)] if u < NY else mx.at[u - NY, h, yy(d)]

    it = {}
    for u in range(U):
        for way, sign in ((0, 1), (1, -1)):
            for s in range(4):
                rows = pl.ds(16 * way, 16) if s == 0 else pl.ds(0, 32)
                it[u, way, s] = remote(
                    own(u, sign * (4 - s) + 8).at[rows],
                    rcv.at[u, way, s, rows],
                    it_s.at[u, way, s],
                    it_r.at[u, way, s],
                    on_feat(0, sign + 8),
                )
    yx = {u: remote(zs.at[u, oh], rzs.at[u], yx_s.at[u], yx_r.at[u], on_feat(1, 0)) for u in range(NY)}
    zz = {
        (k, d): remote(
            tall.at[0, c, k], tall.at[8 - d, c, k], zz_s.at[k, 8 - d], zz_r.at[k, 8 - d], on_z(d)
        )
        for k in range(2)
        for d in range(1, 8)
    }
    cc = {d: remote(tall.at[d, c], tall.at[d, c], cc_s.at[d], cc_r.at[d], core_dev) for d in range(8)}
    st = {
        j: remote(stat, rstat.at[j], st_s.at[j], st_r.at[j], on_feat(a, d)) for j, (a, d) in enumerate(PEERS)
    }
    co = {}
    ct = {}
    for j, (a, d) in enumerate(PEERS):
        dev = on_feat(a, d)
        co[j] = remote(part.at[dev[0]], rpart.at[j], co_s.at[j], co_r.at[j], dev)
        ct[j] = remote(norms.at[dev[0]], rnorms.at[j], ct_s.at[j], ct_r.at[j], dev)

    sent = []

    def start(copy):
        copy.start()
        sent.append(copy)

    def add(to, rows, arrived):
        to[rows] = (to[rows].astype(F32) + arrived.astype(F32)).astype(BF)

    every = pl.ds(0, 32)

    def step(u, s):
        for way, sign in ((0, 1), (1, -1)):
            to = own(u, sign * (4 - s) + 8)
            if u >= NY:
                xu = u - NY
                d = (sign * (4 - s) + 8) % 8
                if s > 0 or way == 0:
                    xx[xu, d].wait_recv()
                    add(to, every, rxx[xu, yy(d)])
            if s > 0:
                it[u, way, s - 1].wait_recv()
                rows = pl.ds(16 * way, 16) if s == 1 else every
                add(to, rows, rcv[u, way, s - 1, rows])
            start(it[u, way, s])

    def transform(rows_sum):
        high = rows_sum.astype(BF)
        low = (rows_sum - high.astype(F32)).astype(BF)
        table = had[...]
        done = jnp.dot(high, table, preferred_element_type=F32) + jnp.dot(low, table, preferred_element_type=F32)
        return (done * (2.0**-9)).astype(BF)

    def gather_step(u):
        if u >= NY:
            xx[u - NY, 0].wait_recv()
        it[u, 0, 3].wait_recv()
        it[u, 1, 3].wait_recv()
        total = own(u, 0)[...].astype(F32) + rcv[u, 0, 3].astype(F32) + rcv[u, 1, 3].astype(F32)
        if u >= NY:
            return total + rxx[u - NY, yy(0)].astype(F32)
        return total

    def finish_y_send(u):
        total = gather_step(u)
        zs[u] = total.reshape(2, 16, W).astype(BF)
        start(yx[u])

    def finish_y(u):
        yx[u].wait_recv()
        total = zs[u, h].astype(F32) + rzs[u].astype(F32)
        proj[pl.ds(16 * u, 16)] = transform(total)

    def finish_x(u):
        row = 16 * NY + 32 * (u - NY)
        proj[pl.ds(row, 32)] = transform(gather_step(u))

    def target_one(k):
        for name in (4, 3, 1):
            for way in range(2):
                start(ty[k, way, name])

    def target_two(k):
        for way, sign in ((0, 1), (1, -1)):
            to = mt.at[k, yy(8 + 2 * sign)]
            ty[k, way, 3].wait_recv()
            ty[k, way, 4].wait_recv()
            add(to, every, rt[k, way, 2])
            add(to, pl.ds(16 * way, 16), rt4[k, way])
            start(ty[k, way, 2])

    def target_across(k):
        total = mt[k, y].astype(F32)
        for name in (1, 2):
            for way in range(2):
                ty[k, way, name].wait_recv()
                total = total + rt[k, way, name - 1].astype(F32)
        zt[k] = total.reshape(2, 16, W).astype(BF)
        for i in (1, 2, 0):
            start(tq[k, i])

    def target_finish(k):
        for i in range(3):
            tq[k, i].wait_recv()
        mine = zt[k, h].astype(F32) + rzt[k, 1].astype(F32)
        other = rzt[k, 0].astype(F32) + rzt[k, 2].astype(F32)
        done = transform(jnp.concatenate([mine, other], axis=0))
        tall[0, c, k, xl] = done[0:16]
        tall[0, c, k, 1 - xl] = done[16:32]
        for d in FAR_FIRST:
            start(zz[k, d])

    def target_rows(pair):
        return jnp.concatenate([tall[d].reshape(128, W) for d in pair], axis=0)

    def target_norms():
        lane = lax.broadcasted_iota(jnp.int32, (256, 128), 1)
        squares = jnp.zeros((256, 128), F32)
        for k, pair in enumerate(PAIRS):
            for d in pair:
                cc[d].wait_recv()
            rows = target_rows(pair).astype(F32)
            norm = jnp.sum(rows * rows, axis=1, keepdims=True)
            high = norm.astype(BF).astype(F32)
            squares = squares + jnp.where(lane == 2 * k, high, 0.0) + jnp.where(lane == 2 * k + 1, norm - high, 0.0)
        moved = jnp.dot(perm[...], squares.astype(BF), preferred_element_type=F32).astype(BF)
        norms[...] = moved.reshape(NF, 16, 128)
        for j in range(len(PEERS)):
            start(ct[j])

    def send_x(u, distances):
        for d in distances:
            start(xx[u, d])

    def forward(d):
        zz[0, 8 - d].wait_recv()
        zz[1, 8 - d].wait_recv()
        start(cc[d])

    loads[1].wait()
    for load in loads[3:]:
        load.start()
    premix(tg_v, 0, store_y(mt.at[0]))
    pl.semaphore_wait(barrier, len(partners))
    target_one(0)
    for d in (2, 6):
        pl.semaphore_signal(far_z, inc=1, device_id=on_z(d), device_id_type=MESH)
    loads[2].wait()
    premix(tg_v, 16, store_y(mt.at[1]))
    target_one(1)
    for u in range(NY):
        loads[3 + u].wait()
        premix(tr_v, 16 * u, store_y(my.at[u]))
        step(u, 0)
    for u in range(NX):
        loads[3 + NY + u].wait()
        for k in range(2):
            premix(tr_v, 16 * NY + 32 * u + 16 * k, store_split(mx.at[u], k))
    send_x(0, FAR_FIRST + (0,))
    send_x(1, FAR_FIRST[:1])
    target_two(0)
    target_two(1)
    tables()
    for u in range(2):
        step(u, 1)
    target_across(0)
    for u in range(2, NY):
        step(u, 1)
    target_across(1)
    send_x(1, FAR_FIRST[1:] + (0,))
    for u in range(NX):
        step(NY + u, 0)
    for u in range(2):
        step(u, 2)
    pl.semaphore_wait(far_z, 2)
    target_finish(0)
    for u in range(2, NY):
        step(u, 2)
    target_finish(1)
    start(cc[0])
    for u in range(NX):
        step(NY + u, 1)
    for u in range(NY):
        step(u, 3)
    for u in range(NX):
        step(NY + u, 2)
    for u in range(NY):
        finish_y_send(u)
    for d in FAR_FIRST[:3]:
        forward(d)
    for u in range(NX):
        step(NY + u, 3)
    for d in FAR_FIRST[3:]:
        forward(d)
    for u in range(NY):
        finish_y(u)
    target_norms()
    for u in range(NX):
        finish_x(NY + u)

    wide = proj[...].astype(F32)
    square = wide * wide
    high = square.astype(BF)
    low = (square - high.astype(F32)).astype(BF)
    ones = jnp.ones((8, W), BF)
    stat[...] = lax.dot_general(ones, high, NT, preferred_element_type=F32) + lax.dot_general(
        ones, low, NT, preferred_element_type=F32
    )
    for j in range(len(PEERS)):
        start(st[j])
    local = jnp.sum(square, axis=1, keepdims=True)
    scaled_t = (wide * lax.rsqrt(local * (1.0 / W) + 1e-30)).astype(BF).T

    for k, pair in enumerate(PAIRS):
        products = jnp.dot(target_rows(pair), scaled_t, preferred_element_type=F32).astype(BF)
        ordered = jnp.dot(perm[...], products, preferred_element_type=F32).astype(BF)
        part[:, pl.ds(16 * k, 16), :] = ordered.reshape(NF, 16, TRAIN)
    for j in range(len(PEERS)):
        start(co[j])

    for copy in sent[: -len(PEERS)]:
        copy.wait_send()
    sums = stat[...]
    for j in range(len(PEERS)):
        st[j].wait_recv()
        sums = sums + rstat[j]
    scale = lax.rsqrt(sums[0:1] * (1.0 / PROJ) + 1e-06)
    eye = lax.broadcasted_iota(jnp.int32, (TRAIN, TRAIN), 0) == lax.broadcasted_iota(jnp.int32, (TRAIN, TRAIN), 1)
    column = jnp.sum(jnp.where(eye, scale, 0.0), axis=1, keepdims=True)
    feat_out[...] = (proj[...].astype(F32) * column).astype(BF)

    def undo(sums):
        mean = sums[0:1] * (1.0 / W) + 1e-30
        return mean * lax.rsqrt(mean)

    norm_sum = norms[f].astype(F32)
    for j in range(len(PEERS)):
        ct[j].wait_recv()
        norm_sum = norm_sum + rnorms[j].astype(F32)
    total = part[f].astype(F32) * undo(stat)
    for j in range(len(PEERS)):
        co[j].wait_recv()
        total = total + rpart[j].astype(F32) * undo(rstat[j])
    total = total * scale
    lane16 = lax.broadcasted_iota(jnp.int32, (16, 128), 1)
    for k, pair in enumerate(PAIRS):
        norm = jnp.sum(jnp.where(lane16 // 2 == k, norm_sum, 0.0), axis=1, keepdims=True)
        factor = lax.rsqrt(norm * (1.0 / PROJ) + 1e-06) * (1.0 / PROJ)
        block = total[16 * k : 16 * k + 16] * factor
        for i, d in enumerate(pair):
            cos_out[pl.ds(pl.multiple_of(((z + d) % 8) * 8, 8), 8), :] = block[8 * i : 8 * i + 8]

    for copy in sent[-len(PEERS) :]:
        copy.wait_send()


def solution(mesh):
    vm = pltpu.VMEM
    dma = pltpu.SemaphoreType.DMA
    n_peers = len(PEERS)
    scratch = [
        vm((TRAIN, 2 * PROJ), BF), vm((32, 2 * PROJ), BF), vm((32, PROJ), jnp.int32), vm((8, PROJ), F32),
        vm((W, W), BF), vm((256, 256), BF),
        vm((2, 8, 32, W), BF), vm((2, 2, 16, W), BF), vm((2, 2, 3, 32, W), BF), vm((2, 2, 16, W), BF), vm((2, 3, 16, W), BF),
        vm((NY, 8, 32, W), BF), vm((NX, 2, 8, 32, W), BF), vm((NX, 8, 32, W), BF), vm((U, 2, 4, 32, W), BF),
        vm((NY, 2, 16, W), BF), vm((NY, 16, W), BF),
        vm((8, 2, 2, 2, 16, W), BF), vm((TRAIN, W), BF),
        vm((8, 128), F32), vm((n_peers, 8, 128), F32),
        vm((NF, 64, 128), BF), vm((n_peers, 64, 128), BF), vm((NF, 16, 128), BF), vm((n_peers, 16, 128), BF),
        dma((3 + U,)), dma((NX, 8)), dma((NX, 8)), dma((2, 2, 4)), dma((2, 2, 4)),
        dma((U, 2, 4)), dma((U, 2, 4)), dma((NY,)), dma((NY,)), dma((2, 3)), dma((2, 3)), dma((2, 8)), dma((2, 8)),
        dma((8,)), dma((8,)), dma((n_peers,)), dma((n_peers,)), dma((n_peers,)), dma((n_peers,)), dma((n_peers,)), dma((n_peers,)),
        pltpu.SemaphoreType.REGULAR,
    ]
    hbm = pl.BlockSpec(memory_space=pl.ANY)
    whole = pl.BlockSpec(memory_space=pltpu.VMEM)

    def local(train_grads, target_grads, signs, block_order):
        features, cosines = pl.pallas_call(
            kernel,
            out_shape=(
                jax.ShapeDtypeStruct((TRAIN, W), BF),
                jax.ShapeDtypeStruct((64, 128), F32),
            ),
            in_specs=[hbm, hbm, hbm, whole],
            out_specs=(whole, whole),
            scratch_shapes=scratch,
            compiler_params=pltpu.CompilerParams(
                collective_id=0, has_side_effects=True, vmem_limit_bytes=int(VML * 2**20)
            ),
        )(train_grads, target_grads, signs, block_order.reshape(1, 32))
        return features, cosines.reshape(32, 2, TRAIN).transpose(2, 0, 1)

    placed = (P("ex", "feat"), P("ex", "feat"), P(), P())
    return jax.shard_map(
        local,
        mesh=mesh,
        in_specs=placed,
        out_specs=(P("ex", "feat"), P("ex", None, "feat")),
        check_vma=False,
    )
```
